32 devices in a mesh: rep: 4 (over z), fsdp: 4 (over y, core), seq: 2 (over x).
Axes of the slice: x: 2, y: 2, z: 4, core: 2. Of those that a mesh axis runs over, the one named last changes fastest.
Arguments:
- tokens: bfloat16 [32, 1024, 1024], P(('rep', 'fsdp'), 'seq'), may hold values from -6 to 6
- cotangent: bfloat16 [32, 1024, 1024], P(('rep', 'fsdp'), 'seq'), may hold values from -6 to 6
- adapter_set: int32 [32], P(('rep', 'fsdp')), may hold values from 0 to 7
- image_live: int32 [32], P(('rep', 'fsdp')), may hold values from 0 to 1, as said below
- first_gain: float32 [1024], replicated, may hold values from 0.5 to 1.5
- first_shift: float32 [1024], replicated, may hold values from -2 to 2
- inproj_weight: bfloat16 [1024, 3072], P('fsdp'), may hold values from -0.1875 to 0.1875
- inproj_bias: float32 [2048], replicated, may hold values from -2 to 2
- outproj_weight: bfloat16 [1024, 1024], P('fsdp'), may hold values from -0.75 to 0.75
- outproj_bias: float32 [1024], replicated, may hold values from -2 to 2
- attend_scale: float32 [1024], replicated, may hold values from 0.5 to 1.5
- second_gain: float32 [1024], replicated, may hold values from 0.5 to 1.5
- second_shift: float32 [1024], replicated, may hold values from -2 to 2
- expand_weight: bfloat16 [1024, 4096], P('fsdp'), may hold values from -0.1875 to 0.1875
- expand_bias: float32 [4096], replicated, may hold values from -2 to 2
- shrink_weight: bfloat16 [4096, 1024], P('fsdp'), may hold values from -0.09375 to 0.09375
- shrink_bias: float32 [1024], replicated, may hold values from -2 to 2
- feedfwd_scale: float32 [1024], replicated, may hold values from 0.5 to 1.5
- inproj_first: float32 [8, 1024, 16], replicated, may hold values from -0.1875 to 0.1875
- inproj_second: float32 [8, 16, 3072], replicated, may hold values from -0.75 to 0.75
- outproj_first: float32 [8, 1024, 16], replicated, may hold values from -0.1875 to 0.1875
- outproj_second: float32 [8, 16, 1024], replicated, may hold values from -0.75 to 0.75
- expand_first: float32 [8, 1024, 16], replicated, may hold values from -0.1875 to 0.1875
- expand_second: float32 [8, 16, 4096], replicated, may hold values from -0.75 to 0.75
- shrink_first: float32 [8, 4096, 16], replicated, may hold values from -0.1875 to 0.1875
- shrink_second: float32 [8, 16, 1024], replicated, may hold values from -0.75 to 0.75
Outputs:
- block_output: bfloat16 [32, 1024, 1024], P(('rep', 'fsdp'), 'seq')
- input_grad: bfloat16 [32, 1024, 1024], P(('rep', 'fsdp'), 'seq')
- inproj_first_grad: float32 [8, 1024, 16], replicated
- inproj_second_grad: float32 [8, 16, 3072], replicated
- outproj_first_grad: float32 [8, 1024, 16], replicated
- outproj_second_grad: float32 [8, 16, 1024], replicated
- expand_first_grad: float32 [8, 1024, 16], replicated
- expand_second_grad: float32 [8, 16, 4096], replicated
- shrink_first_grad: float32 [8, 4096, 16], replicated
- shrink_second_grad: float32 [8, 16, 1024], replicated
The draws below stay inside these ranges and needn't reach their ends.
Inputs may be any that keep to these rules, and one draw needn't show every extreme that they name: `image_live`: image slots come in groups of 2 consecutive ones, one group for each index pair of rep and fsdp; in each group the live slots come first, at least one is live, and in some group all 2 are live.
All inputs are finite; a program needn't handle non-finite values.
Results may differ from the reference program's by a relative error of at most 0.018.
The reference program's roundings to bfloat16 on the way count: a program that leaves them out, or rounds other values in their place, can miss the bound.
Values may be sent and summed in bfloat16 or wider, within the bound.
A program may use at most 320 MiB of HBM per device.

```python
import math
import jax
import jax.numpy as jnp
from jax import lax

D = 1024
FF = 4096
HEADS = 16
HEAD_DIM = 64
RANK = 16
SETS = 8
SEQLEN = 1024
SLOTS = 2
IMAGES = 32
N_SEQ = 2


def draw_image_live(key, part):
    key = jax.random.fold_in(key, 7)
    group_count = IMAGES // SLOTS
    count_key, full_key = jax.random.split(key)
    counts = jax.random.randint(count_key, (group_count,), 1, SLOTS + 1)
    chosen = jax.random.randint(full_key, (), 0, group_count)
    counts = jnp.where(jnp.arange(group_count) == chosen, SLOTS, counts)
    flags = jnp.arange(SLOTS)[None, :] < counts[:, None]
    return flags.astype(jnp.int32).reshape(IMAGES)


def touch_ends(values, own_key, smallest, top_value):
    longest = values.shape.index(max(values.shape))
    spots = []
    for shift in (0, 1):
        where = [jax.random.randint(jax.random.fold_in(own_key, axis), (), 0, length) for axis, length in enumerate(values.shape)]
        where[longest] = (where[longest] + shift) % values.shape[longest]
        spots.append(tuple(where))
    return values.at[spots[0]].set(smallest).at[spots[1]].set(top_value)


def level_of(own_key, dims, shards, least, largest):
    level, own = 1.0, jax.random.fold_in(own_key, 6)
    for axis_at, parts in shards:
        heights = jnp.exp(jax.random.uniform(jax.random.fold_in(own, axis_at), (parts,), jnp.float32, least / len(shards), largest / len(shards)))
        level = level * jnp.repeat(heights, dims[axis_at] // parts).reshape([-1 if axis == axis_at else 1 for axis in range(len(dims))])
    return level


def normal_values(own_key, dims, deviation, most, cuts=(), dtype=jnp.bfloat16):
    factor_of = level_of(own_key, dims, cuts, -0.22, 0.18) if cuts else 1.0
    values = jax.random.normal(own_key, dims, jnp.float32) * deviation * factor_of
    return jnp.minimum(jnp.maximum(values, -most), most).astype(dtype)


def setup_inputs(seed: int = 0) -> dict:
    splits = jax.random.split(jax.random.key(seed), 27)
    return {
        "tokens": normal_values(splits[0], (IMAGES, SEQLEN, D), 1.0, 6.0, ((0, 16), (1, 2))),
        "cotangent": normal_values(splits[1], (IMAGES, SEQLEN, D), 1.0, 6.0, ((0, 16), (1, 2))),
        "adapter_set": touch_ends(jax.random.randint(splits[2], (IMAGES,), 0, SETS), jax.random.fold_in(splits[2], 1), 0, SETS - 1).astype(jnp.int32),
        "image_live": draw_image_live(jax.random.fold_in(splits[26], 71), 0),
        "first_gain": jnp.clip(1.0 + 0.1 * jax.random.normal(splits[4], (D,), jnp.float32), 0.5, 1.5),
        "first_shift": normal_values(splits[5], (D,), 0.3, 2.0, (), jnp.float32),
        "inproj_weight": normal_values(splits[6], (D, 3 * D), D ** -0.5, 0.1875, ((0, 4),)),
        "inproj_bias": normal_values(splits[7], (2 * D,), 0.3, 2.0, (), jnp.float32),
        "outproj_weight": normal_values(splits[8], (D, D), (D // 16) ** -0.5, 0.75, ((0, 4),)),
        "outproj_bias": normal_values(splits[9], (D,), 0.3, 2.0, (), jnp.float32),
        "attend_scale": jnp.clip(jnp.exp(jax.random.uniform(splits[10], (D,), jnp.float32, math.log(0.5), math.log(1.5))), 0.5, 1.5),
        "second_gain": jnp.clip(1.0 + 0.1 * jax.random.normal(splits[11], (D,), jnp.float32), 0.5, 1.5),
        "second_shift": normal_values(splits[12], (D,), 0.3, 2.0, (), jnp.float32),
        "expand_weight": normal_values(splits[13], (D, FF), D ** -0.5, 0.1875, ((0, 4),)),
        "expand_bias": normal_values(splits[14], (FF,), 0.3, 2.0, (), jnp.float32),
        "shrink_weight": normal_values(splits[15], (FF, D), FF ** -0.5, 0.09375, ((0, 4),)),
        "shrink_bias": normal_values(splits[16], (D,), 0.3, 2.0, (), jnp.float32),
        "feedfwd_scale": jnp.clip(jnp.exp(jax.random.uniform(splits[17], (D,), jnp.float32, math.log(0.5), math.log(1.5))), 0.5, 1.5),
        "inproj_first": normal_values(splits[18], (SETS, D, RANK), D ** -0.5, 0.1875, (), jnp.float32),
        "inproj_second": normal_values(splits[19], (SETS, RANK, 3 * D), (4 * RANK) ** -0.5, 0.75, (), jnp.float32),
        "outproj_first": normal_values(splits[20], (SETS, D, RANK), D ** -0.5, 0.1875, (), jnp.float32),
        "outproj_second": normal_values(splits[21], (SETS, RANK, D), (4 * RANK) ** -0.5, 0.75, (), jnp.float32),
        "expand_first": normal_values(splits[22], (SETS, D, RANK), D ** -0.5, 0.1875, (), jnp.float32),
        "expand_second": normal_values(splits[23], (SETS, RANK, FF), (4 * RANK) ** -0.5, 0.75, (), jnp.float32),
        "shrink_first": normal_values(splits[24], (SETS, FF, RANK), (FF // 4) ** -0.5, 0.1875, (), jnp.float32),
        "shrink_second": normal_values(splits[25], (SETS, RANK, D), (4 * RANK) ** -0.5, 0.75, (), jnp.float32),
    }


@jax.custom_vjp
def low(v):
    return lax.optimization_barrier(v.astype(jnp.bfloat16)).astype(jnp.float32)

@jax.custom_vjp
def low_back(v):
    return v

def low_keep(v):
    return (low(v), None)

def low_pass(kept, grad):
    return (grad,)

def back_keep(v):
    return (v, None)

def back_low(kept, grad):
    return (low(grad),)
low.defvjp(low_keep, low_pass)
low_back.defvjp(back_keep, back_low)
highest = lax.Precision.HIGHEST
epsilon = 1e-06

def matmul(left, right):
    return jnp.dot(left, right, precision=highest)

def round_both(value):
    return low_back(low(value))

def layer_norm(values, gain, shift):
    center = values - lax.optimization_barrier(jnp.mean(values, axis=-1, keepdims=True))
    spread = lax.optimization_barrier(jnp.mean(center * center, axis=-1, keepdims=True))
    return center * lax.rsqrt(spread + epsilon) * gain + shift

def attend_block(query_block, key_rows, value_rows):
    length = query_block.shape[0]
    key_used = key_rows.reshape(SEQLEN, HEADS, HEAD_DIM)
    value_used = value_rows.reshape(SEQLEN, HEADS, HEAD_DIM)
    query_heads = query_block.reshape(length, HEADS, HEAD_DIM)
    scores = jnp.einsum('qhe,khe->hqk', query_heads, key_used, precision=highest) * 0.125
    scores = low_back(scores)
    top = lax.optimization_barrier(jnp.max(scores, axis=-1, keepdims=True))
    expo = jnp.exp(scores - top)
    attention = low(expo / lax.optimization_barrier(jnp.sum(expo, axis=-1, keepdims=True)))
    mixed = jnp.einsum('hqk,khe->qhe', attention, value_used, precision=highest)
    return mixed.reshape(length, HEADS * HEAD_DIM)

def image_layer(values, set_index, live_flag, adapters, frozen):
    first_gain, first_shift, inproj_weight, inproj_bias, outproj_weight, outproj_bias, attend_scale, second_gain, second_shift, expand_weight, expand_bias, shrink_weight, shrink_bias, feedfwd_scale = frozen
    picked = [low_front(table[set_index]) for table in adapters]
    width = values.shape[-1]
    normed_one = low(layer_norm(values, first_gain, first_shift))
    enter_low = round_both(matmul(normed_one, picked[0]))
    bias_full = jnp.concatenate([inproj_bias[:width], jnp.zeros((width,), jnp.float32), inproj_bias[width:]])
    joined = matmul(normed_one, inproj_weight) + bias_full + 2.0 * matmul(enter_low, picked[1])
    queries = round_both(joined[:, :width])
    key_rows = round_both(joined[:, width:2 * width])
    value_rows = round_both(joined[:, 2 * width:])
    query_blocks = queries.reshape(N_SEQ, SEQLEN // N_SEQ, width)

    def one_block(query_block):
        return attend_block(query_block, key_rows, value_rows)
    attended = lax.map(jax.checkpoint(one_block), query_blocks).reshape(SEQLEN, width)
    attended = round_both(attended)
    leave_low = round_both(matmul(attended, picked[2]))
    branch = low_back(matmul(attended, outproj_weight) + outproj_bias + 2.0 * matmul(leave_low, picked[3]))
    middle = values + attend_scale * branch
    normed_two = low(layer_norm(middle, second_gain, second_shift))
    widen_low = round_both(matmul(normed_two, picked[4]))
    before = low_back(matmul(normed_two, expand_weight) + expand_bias + 2.0 * matmul(widen_low, picked[5]))
    hidden = round_both(jax.nn.gelu(before, approximate=False))
    narrow_low = round_both(matmul(hidden, picked[6]))
    feed = low_back(matmul(hidden, shrink_weight) + shrink_bias + 2.0 * matmul(narrow_low, picked[7]))
    result = middle + feedfwd_scale * feed
    return result * live_flag

def low_front(value):
    return low(value)

def reference(tokens, cotangent, adapter_set, image_live, first_gain, first_shift, inproj_weight, inproj_bias, outproj_weight, outproj_bias, attend_scale, second_gain, second_shift, expand_weight, expand_bias, shrink_weight, shrink_bias, feedfwd_scale, inproj_first, inproj_second, outproj_first, outproj_second, expand_first, expand_second, shrink_first, shrink_second):
    frozen = tuple((item.astype(jnp.float32) for item in (first_gain, first_shift, inproj_weight, inproj_bias, outproj_weight, outproj_bias, attend_scale, second_gain, second_shift, expand_weight, expand_bias, shrink_weight, shrink_bias, feedfwd_scale)))
    adapters = (inproj_first, inproj_second, outproj_first, outproj_second, expand_first, expand_second, shrink_first, shrink_second)
    inputs = tokens.astype(jnp.float32)
    live_flags = image_live.astype(jnp.float32)

    def forward(inputs_all, adapter_tables):

        def one_image(packed):
            values, set_index, live_flag = packed
            return image_layer(values, set_index, live_flag, adapter_tables, frozen)
        return lax.map(jax.checkpoint(one_image), (inputs_all, adapter_set, live_flags))
    output, pullback = jax.vjp(forward, inputs, adapters)
    grad_inputs, grad_tables = pullback(cotangent.astype(jnp.float32))
    return (output.astype(jnp.bfloat16), grad_inputs.astype(jnp.bfloat16), grad_tables[0], grad_tables[1], grad_tables[2], grad_tables[3], grad_tables[4], grad_tables[5], grad_tables[6], grad_tables[7])
```

```python
import functools
import math

import jax
import jax.numpy as jnp
from jax import lax
from jax.experimental import pallas as pl
from jax.experimental.pallas import tpu as pltpu
from jax.sharding import PartitionSpec as P

HEAD_DIM = 64
LANES = 128
epsilon = 1e-06

low = jnp.bfloat16
wide = jnp.float32


def dot_nn(left, right):
    return lax.dot_general(left, right, (((1,), (0,)), ((), ())), preferred_element_type=wide)


def dot_nt(left, right):
    return lax.dot_general(left, right, (((1,), (1,)), ((), ())), preferred_element_type=wide)


def dot_tn(left, right):
    return lax.dot_general(left, right, (((0,), (0,)), ((), ())), preferred_element_type=wide)


def normal_rows(values):
    center = values - jnp.mean(values, axis=-1, keepdims=True)
    spread = jnp.mean(center * center, axis=-1, keepdims=True)
    inverse = lax.rsqrt(spread + epsilon)
    return center * inverse, inverse


def layer_norm(values, gain, shift):
    return normal_rows(values)[0] * gain + shift


def layer_norm_back(gradient, values, gain):
    unit, inverse = normal_rows(values)
    scaled = gradient * gain
    mean_one = jnp.mean(scaled, axis=-1, keepdims=True)
    mean_two = jnp.mean(scaled * unit, axis=-1, keepdims=True)
    return inverse * (scaled - mean_one - unit * mean_two)


def for_rows(length, tile, body, start=0):
    def step(index, carry):
        body(pl.ds(pl.multiple_of(start + index * tile, tile), tile))
        return carry

    lax.fori_loop(0, length // tile, step, 0)


def attend_pairs(planes, out_ref, rest_ref, lse_ref, tile, splits=4):
    length = planes[0][0].shape[0]
    lane = lax.broadcasted_iota(jnp.int32, (1, LANES), 1)
    is_first = lane < HEAD_DIM
    size = length // splits
    keys, values, units = [], [], []
    for pair, (_, k_ref, v_ref) in enumerate(planes):
        keys.append([k_ref[n * size : (n + 1) * size, :] for n in range(splits)])
        values.append([])
        for n in range(splits):
            value = v_ref[n * size : (n + 1) * size, :]
            one = jnp.ones_like(value)
            values[pair].append((jnp.where(is_first, value, one), jnp.where(is_first, one, value)))
        units += [(pair, start, head) for start in range(0, length, tile) for head in range(2)]
    scores, tops, expos, products = {}, {}, {}, {}

    def finish(pair, start):
        rows = pl.ds(start, tile)
        mixed = [products.pop((pair, start, head)) for head in range(2)]
        total = jnp.where(
            is_first, pltpu.roll(mixed[0], HEAD_DIM, 1), pltpu.roll(mixed[1], HEAD_DIM, 1)
        )
        attended = jnp.where(is_first, mixed[0], mixed[1]) / total
        rounded = attended.astype(low)
        out_ref[pair, rows, :] = rounded
        rest_ref[pair, rows, :] = (attended - rounded.astype(wide)).astype(low)
        top = jnp.where(is_first, tops.pop((pair, start, 0)), tops.pop((pair, start, 1)))
        lse_ref[pair, rows, :] = top + jnp.log(total)

    for turn in range(len(units) + 2):
        if turn < len(units):
            pair, start, head = units[turn]
            query = planes[pair][0][pl.ds(start, tile), :] * low(0.125)
            zero = jnp.zeros_like(query)
            query = jnp.where(is_first, query, zero) if head == 0 else jnp.where(is_first, zero, query)
            highest = None
        for n in range(splits):
            if turn < len(units):
                part = dot_nt(query, keys[pair][n])
                scores[turn, n] = part
                for i in range(0, size, LANES):
                    column = part[:, i : i + LANES]
                    highest = column if highest is None else jnp.maximum(highest, column)
            if 0 <= turn - 1 < len(units):
                expo = jnp.exp(scores.pop((turn - 1, n)) - tops[units[turn - 1]])
                expos[turn - 1, n] = expo.astype(low)
        if turn < len(units):
            tops[units[turn]] = jnp.max(highest, axis=-1, keepdims=True)
        if turn >= 2:
            unit = units[turn - 2]
            expo = jnp.concatenate([expos.pop((turn - 2, n)) for n in range(splits)], axis=1)
            value = jnp.concatenate([values[unit[0]][n][unit[2]] for n in range(splits)], axis=0)
            products[unit] = dot_nn(expo, value)
            if unit[2] == 1:
                finish(*unit[:2])


def front_kernel(set_ref, tokens_ref, cot_ref, w0_ref, w1_ref, w2_ref, w3_ref, gain_ref, shift_ref,
                 bias_ref, table_refs,
                 x_out, c_out, g0_ref, g1_ref, g2_ref, g4_ref, normed_out, joined_out, low_ref,
                 picked_refs, att_ref, rest_ref, lse_ref,
                 x_s, c_s, normed_s, weight_s, joined_s, ow_s, ew_s, far_s, table_s, send_sem, recv_sem,
                 local_sem, *, sizes, tile, per):
    step = pl.program_id(0)
    steps = pl.num_programs(0) - 1
    count = sizes["seq"]
    lines = sizes["fsdp"] // 2
    rep, line = lax.axis_index("rep"), lax.axis_index("fsdp")
    seq = lax.axis_index("seq")
    core = lax.rem(line, 2)
    row = lax.div(line, 2)
    half = lax.rem(rep, 2)
    sibling = {"fsdp": line + 1 - 2 * core}
    pair = {"rep": rep + 1 - 2 * half}
    part = tokens_ref.shape[1]
    chunks, _, chunk = weight_s.shape
    tiles = chunk // LANES
    sends, locals_ = [], []

    def remote(source, target, device):
        position = len(sends)
        sends.append(
            pltpu.make_async_remote_copy(
                src_ref=source,
                dst_ref=target,
                send_sem=send_sem.at[position],
                recv_sem=recv_sem.at[position],
                device_id=device,
                device_id_type=pl.DeviceIdType.MESH,
            )
        )
        return sends[-1]

    def local(source, target):
        position = len(locals_)
        locals_.append(pltpu.make_async_copy(source, target, local_sem.at[position]))
        return locals_[-1]

    across = []
    for shift in range(1, lines):
        across.append(
            (
                {"fsdp": lax.rem(row + shift, lines) * 2 + core},
                lax.rem(row + lines - shift, lines) * 2 + core,
            )
        )
    around = [{"seq": lax.rem(seq + shift, count)} for shift in range(1, count)]

    def columns_of(shard, whole, start, size, chunked):
        height = shard.shape[0] // 2

        def own(which):
            return shard.at[pl.ds(which * height, height), pl.ds(start, size)]

        def placed(which_line, which):
            at = pl.multiple_of(which_line * 2 * height + which * height, height)
            if chunked:
                return whole.at[start // size, pl.ds(at, height), :]
            return whole.at[pl.ds(at, height), :]

        return own, placed

    def travel(own, placed):
        first, along, over, over_late = [], [], [], []
        for target, origin in across:
            first.append(remote(own(half), placed(line, half), target))
            along.append(remote(placed(origin, half), placed(origin, half), pair))
            over.append(remote(placed(origin, half), placed(origin, half), sibling))
            over_late.append(remote(placed(origin, 1 - half), placed(origin, 1 - half), sibling))
        return first, along, over, over_late

    def begin(copies):
        for copy in copies:
            copy.start()

    def arrived(copies):
        for copy in copies:
            copy.wait_recv()

    early, early_own = [], []
    for j in range(chunks):
        early.append(travel(*columns_of(w0_ref, weight_s, j * chunk, chunk, True)))
        height = w0_ref.shape[0]
        source = w0_ref.at[:, pl.ds(j * chunk, chunk)]
        target = weight_s.at[j, pl.ds(pl.multiple_of(line * height, height), height), :]
        early_own.append((remote(source, target, sibling), local(source, target)))
    late = [travel(*columns_of(w1_ref, ow_s, 0, w1_ref.shape[1], False))]
    splits = ew_s.shape[0]
    size = ew_s.shape[2]
    for j in range(splits):
        late.append(travel(*columns_of(w2_ref, ew_s, j * size, size, True)))
    deep = w3_ref.shape[0] // 4
    source = w3_ref.at[pl.ds(pl.multiple_of(half * deep, deep), deep), :]
    shrink_far = [
        remote(source, far_s.at[i], target) for i, (target, _) in enumerate(across)
    ]
    far_store = local(far_s, g4_ref)
    height = w1_ref.shape[0]
    mine = pl.ds(pl.multiple_of(line * height, height), height)
    late_own = [(remote(w1_ref, ow_s.at[mine, :], sibling), local(w1_ref, ow_s.at[mine, :]))]
    late_store = [local(ow_s, g1_ref)]
    for j in range(splits):
        source, target = w2_ref.at[:, pl.ds(j * size, size)], ew_s.at[j, mine, :]
        late_own.append((remote(source, target, sibling), local(source, target)))
        late_store.append(local(ew_s.at[j], g2_ref.at[j]))
    group = [0] + [1 + splits * i // 4 for i in range(1, 5)]

    def pass_on(pieces):
        for piece in pieces:
            arrived(piece[0])
            begin(piece[1])
            begin(piece[2])

    def pass_over(pieces):
        for piece in pieces:
            arrived(piece[1])
            begin(piece[3])

    def exchange(source, target):
        moves = []
        for shift, device in enumerate(around, 1):
            moves.append(
                remote(source.at[device["seq"]], target.at[pl.ds(shift * part, part), :], device)
            )
        return moves, local(source.at[seq], target.at[pl.ds(0, part), :])

    x_moves, x_own = exchange(tokens_ref, x_s)
    c_moves = [
        remote(cot_ref.at[device["seq"]], c_s.at[pl.ds((shift - 1) * part, part), :], device)
        for shift, device in enumerate(around, 1)
    ]
    c_store = local(c_s, c_out)
    table_loads = [local(table, held) for table, held in zip(table_refs, table_s)]
    x_store = local(x_s, x_out)
    normed_store = local(normed_s, normed_out)
    weight_store = local(weight_s, g0_ref)
    joined_store = local(joined_s, joined_out)

    assert (len(sends), len(locals_)) == (send_sem.shape[0], local_sem.shape[0])

    def take_tables(start, stop):
        which = set_ref[seq]
        for load, held, picked in zip(
            table_loads[start:stop], table_s[start:stop], picked_refs[start:stop]
        ):
            load.wait()
            picked[...] = held[which].astype(low)

    @pl.when(step == 0)
    def _():
        x_own.start()
        begin(table_loads[:2])
        barrier = pltpu.get_barrier_semaphore()
        peers = [sibling, pair, *around, *(target for target, _ in across)]
        for peer in peers:
            pl.semaphore_signal(barrier, inc=1, device_id=peer, device_id_type=pl.DeviceIdType.MESH)
        pl.semaphore_wait(barrier, len(peers))
        begin(early[0][0])
        begin(early[1][0])
        begin(x_moves)
        for j in range(chunks):
            early_own[j][0].start()
            early_own[j][1].start()
        take_tables(0, 2)
        first_ref, second_ref = picked_refs[:2]
        first = first_ref[...]

        def norm(start):
            def run(rows):
                normed = layer_norm(x_s[rows, :].astype(wide), gain_ref[...], shift_ref[...])
                normed = normed.astype(low)
                normed_s[rows, :] = normed
                low_ref[rows, :] = dot_nt(normed, first).astype(low)

            for_rows(part, tile, run, start)

        def project(j, start, length):
            columns = slice(j * chunk, (j + 1) * chunk)
            plane = j * chunk // x_s.shape[1]
            shift = max(plane - 1, 0) * x_s.shape[1]
            second = second_ref[:, columns]

            def run(rows):
                joined = dot_nn(normed_s[rows, :], weight_s[j])
                if plane != 1:
                    joined += bias_ref[:, columns.start - shift : columns.stop - shift]
                joined = (joined + 2.0 * dot_nn(low_ref[rows, :], second)).astype(low)
                for i in range(tiles):
                    joined_s[j * tiles + i, rows, :] = joined[:, i * LANES : (i + 1) * LANES]

            for_rows(length, tile, run, start)

        x_own.wait()
        norm(0)
        for turn in range(chunks + 2):
            if turn < chunks:
                arrived(early[turn][0])
                begin(early[turn][1])
                begin(early[turn][2])
                if turn + 2 < chunks:
                    begin(early[turn + 2][0])
                else:
                    begin(late[turn + 2 - chunks][0])
            if 0 <= turn - 1 < chunks:
                arrived(early[turn - 1][1])
                begin(early[turn - 1][3])
            if turn >= 2:
                j = turn - 2
                early_own[j][1].wait()
                arrived([early_own[j][0]])
                arrived(early[j][2])
                arrived(early[j][3])
                project(j, 0, part)
        for piece in late[2:]:
            begin(piece[0])
        begin(shrink_far)
        begin(table_loads[2:])
        for over, own in late_own:
            over.start()
            own.start()
        weight_store.start()
        for shift, move in enumerate(x_moves, 1):
            move.wait_recv()
            norm(shift * part)
        x_store.start()
        normed_store.start()
        for j in range(chunks):
            project(j, part, part * (count - 1))
        joined_store.start()
        pass_on(late[: group[1]])
        begin(c_moves)

    @pl.when(step == 2)
    def _():
        pass_on(late[group[1] : group[2]])

    @pl.when(step == 3)
    def _():
        pass_on(late[group[2] : group[3]])
        pass_over(late[: group[1]])

    @pl.when(step == 4)
    def _():
        pass_on(late[group[3] :])
        pass_over(late[group[1] : group[2]])

    @pl.when(step > 0)
    def _():
        pairs = joined_s.shape[0] // 3
        at = [(step - 1) * per + i for i in range(per)]
        attend_pairs(
            [
                (joined_s.at[i], joined_s.at[i + pairs], joined_s.at[i + 2 * pairs])
                for i in at
            ],
            att_ref,
            rest_ref,
            lse_ref,
            min(joined_s.shape[1], tile),
        )

    @pl.when(step == steps)
    def _():
        take_tables(2, len(table_loads))
        arrived(c_moves)
        c_store.start()
        arrived(shrink_far)
        far_store.start()
        pass_over(late[group[2] :])
        for over, own in late_own:
            over.wait_recv()
            own.wait()
        for piece, store in zip(late, late_store):
            arrived(piece[2])
            arrived(piece[3])
            store.start()
        for store in (*late_store, c_store, far_store):
            store.wait()
        for store in (x_store, normed_store, weight_store, joined_store):
            store.wait()
        for copy in sends:
            copy.wait_send()


def front(sizes, sets, tokens, cotangent, gain, shift, bias, weights, tables, tile=256):
    count, part, width = tokens.shape
    length = count * part
    rank, columns = tables[1].shape[1:]
    splits = 2 * sizes["fsdp"]
    expand = (splits, width, weights[2].shape[1] // splits)
    far = (length - part, width)
    pairs = width // LANES
    chunks = 6
    lines = sizes["fsdp"] // 2
    far_rows = (lines - 1, weights[3].shape[0] // 4, width)
    remotes = (lines - 1) * (4 * (chunks + 1 + splits) + 1) + chunks + 1 + splits + 2 * (count - 1)
    anywhere = pl.BlockSpec(memory_space=pl.ANY)
    once = pl.Buffered(1)

    def resident(shape):
        return pl.BlockSpec(shape, lambda i: (0,) * len(shape), pipeline_mode=once)

    per = 2
    planes = (pairs, length, LANES)
    block = pl.BlockSpec((per, length, LANES), lambda i: (jnp.maximum(i - 1, 0), 0, 0))
    image = jax.ShapeDtypeStruct((length, width), low)
    return pl.pallas_call(
        functools.partial(front_kernel, sizes=sizes, tile=min(tile, part), per=per),
        grid=(pairs // per + 1,),
        in_specs=[
            pl.BlockSpec(memory_space=pltpu.SMEM),
            *[anywhere] * 6,
            resident((1, width)),
            resident((1, width)),
            resident(bias.shape),
            [pl.BlockSpec(memory_space=pltpu.HBM)] * len(tables),
        ],
        out_specs=[
            *[anywhere] * 8,
            resident((length, rank)),
            [resident(table.shape[1:]) for table in tables],
            block,
            block,
            block,
        ],
        out_shape=[
            image,
            jax.ShapeDtypeStruct(far, low),
            jax.ShapeDtypeStruct((chunks, width, columns // chunks), low),
            jax.ShapeDtypeStruct((width, width), low),
            jax.ShapeDtypeStruct(expand, low),
            jax.ShapeDtypeStruct(far_rows, low),
            image,
            jax.ShapeDtypeStruct((columns // LANES, length, LANES), low),
            jax.ShapeDtypeStruct((length, rank), low),
            [jax.ShapeDtypeStruct(table.shape[1:], low) for table in tables],
            jax.ShapeDtypeStruct(planes, low),
            jax.ShapeDtypeStruct(planes, low),
            jax.ShapeDtypeStruct(planes, wide),
        ],
        scratch_shapes=[
            pltpu.VMEM((length, width), low),
            pltpu.VMEM(far, low),
            pltpu.VMEM((length, width), low),
            pltpu.VMEM((chunks, width, columns // chunks), low),
            pltpu.VMEM((columns // LANES, length, LANES), low),
            pltpu.VMEM((width, width), low),
            pltpu.VMEM(expand, low),
            pltpu.VMEM(far_rows, low),
            [pltpu.VMEM(table.shape, wide) for table in tables],
            pltpu.SemaphoreType.DMA((remotes,)),
            pltpu.SemaphoreType.DMA((remotes,)),
            pltpu.SemaphoreType.DMA((chunks + 9 + 2 * splits + len(tables),)),
        ],
        compiler_params=pltpu.CompilerParams(
            vmem_limit_bytes=61 << 20, collective_id=0, has_side_effects=True
        ),
        cost_estimate=pl.CostEstimate(
            flops=2 * length * width * columns + 16 * length * length * width,
            bytes_accessed=4 * width * (columns + 4 * length),
            transcendentals=length * length * width // HEAD_DIM,
        ),
        name="front",
    )(sets, tokens, cotangent, *weights, gain, shift, bias, list(tables))


def three_parts(values):
    high = values.astype(low)
    rest = values - high.astype(wide)
    middle = rest.astype(low)
    return high, middle, (rest - middle.astype(wide)).astype(low)


def attend_back_pair(q_ref, k_ref, v_ref, g_ref, o_ref, r_ref, lse_ref, out_ref, start, q_cols,
                     g_cols, key_sum, value_sum, tile, splits=4):
    columns = pl.ds(start, LANES)
    length = q_ref.shape[0]
    lane = lax.broadcasted_iota(jnp.int32, (1, LANES), 1)
    is_first = lane < HEAD_DIM
    size = length // splits
    q_cols[...] = jnp.transpose(q_ref[...] * low(0.125))
    g_cols[...] = jnp.transpose(g_ref[...])
    sides = {}
    for head in range(2):
        mine = is_first if head == 0 else ~is_first
        base = HEAD_DIM if head == 0 else 0
        ones = jnp.where((lane >= base) & (lane < base + 3), 1.0, 0.0).astype(low)
        for n in range(splits):
            key = k_ref[n * size : (n + 1) * size, :]
            value = v_ref[n * size : (n + 1) * size, :]
            sides[head, n] = (
                jnp.where(mine, key, ones),
                jnp.where(mine, value, ones),
                jnp.where(mine, key, jnp.zeros_like(key)),
            )

    def extend(head, rows_value, column):
        base = HEAD_DIM if head == 0 else 0
        high, middle, last = three_parts(column)
        pieces = jnp.where(
            lane == base,
            high,
            jnp.where(lane == base + 1, middle, jnp.where(lane == base + 2, last, low(0.0))),
        )
        return jnp.where(is_first if head == 0 else ~is_first, rows_value, pieces)

    def sides_of(begin, head):
        rows = pl.ds(begin, tile)
        grads = g_ref[rows, :]
        product = grads.astype(wide) * (o_ref[rows, :].astype(wide) + r_ref[rows, :].astype(wide))
        mine = is_first if head == 0 else ~is_first
        inner = jnp.sum(jnp.where(mine, product, 0.0), axis=-1, keepdims=True)
        logsum = lse_ref[rows, head * HEAD_DIM : head * HEAD_DIM + 1]
        return (
            extend(head, q_ref[rows, :] * low(0.125), -logsum),
            extend(head, grads, -inner),
        )

    units = [
        (begin, head, n)
        for begin in range(0, length, tile)
        for head in range(2)
        for n in range(splits)
    ]
    raw, made, query_grad = {}, {}, {}
    for turn in range(len(units) + 2):
        if turn < len(units):
            begin, head, n = units[turn]
            if n == 0:
                left = sides_of(begin, head)
            side = sides[head, n]
            raw[turn] = dot_nt(left[0], side[0]), dot_nt(left[1], side[1])
        if 0 <= turn - 1 < len(units):
            scores, change = raw.pop(turn - 1)
            probs = jnp.exp(scores)
            made[turn - 1] = probs.astype(low), (probs * change).astype(low)
        if turn >= 2:
            begin, head, n = units[turn - 2]
            prob_low, grad_scores = made.pop(turn - 2)
            span = slice(head * HEAD_DIM, (head + 1) * HEAD_DIM)
            rows = slice(begin, begin + tile)
            across = slice(n * size, (n + 1) * size)
            value_term = dot_nn(g_cols[span, rows], prob_low)
            key_term = dot_nn(q_cols[span, rows], grad_scores)
            if begin == 0:
                value_sum[span, across] = value_term
                key_sum[span, across] = key_term
            else:
                value_sum[span, across] += value_term
                key_sum[span, across] += key_term
            term = dot_nn(grad_scores, sides[head, n][2])
            query_grad[begin] = term if begin not in query_grad else query_grad[begin] + term
            if head == 1 and n == splits - 1:
                out_ref[0, rows, columns] = (query_grad.pop(begin) * 0.125).astype(low)
    out_ref[1, :, columns] = jnp.transpose(key_sum[...]).astype(low)
    out_ref[2, :, columns] = jnp.transpose(value_sum[...]).astype(low)


def join_planes(ref, rows):
    return jnp.concatenate([ref[i, rows, :] for i in range(ref.shape[0])], axis=1)


def feed_kernel(set_ref, live_ref, x_hbm, att_hbm, cot_ref, far_ref, obias_ref, oscale_ref, gain_ref,
                shift_ref, ebias_ref, sbias_ref, fscale_ref, ow_hbm, ew_ref, shard_ref, first_ref, o1_ref, o2_ref,
                e1_ref, e2_ref, s1_ref, s2_ref,
                result_out, gmid_out, gatt_out, terms_ref,
                x_ref, att_ref, ow_ref, middle_s, normed_s, gfeed_s, feed_s, gnormed_s, ew_s, sw_s, cot_s, result_ref, gmid_ref, gatt_ref, leave_s, widen_s,
                gnarrow_s, narrow_s, gwiden_s, to1_ref, to2_ref,
                te1_ref, te2_ref, ts1_ref, ts2_ref, send_sem, recv_sem, local_sem, out_sem, in_sem, *, sizes, tile,
                group):
    step = pl.program_id(0)
    steps = sizes["fsdp"]
    lines = steps // 2
    line, seq = lax.axis_index("fsdp"), lax.axis_index("seq")
    core = lax.rem(line, 2)
    row = lax.div(line, 2)
    sibling = {"fsdp": line + 1 - 2 * core}
    length, width = x_ref.shape
    tiles = width // LANES
    chunk = shard_ref.shape[0]
    block = chunk // 2
    live = live_ref[seq].astype(wide)
    sends, locals_ = [], []

    def remote(source, target, device):
        position = len(sends)
        sends.append(
            pltpu.make_async_remote_copy(
                src_ref=source,
                dst_ref=target,
                send_sem=send_sem.at[position],
                recv_sem=recv_sem.at[position],
                device_id=device,
                device_id_type=pl.DeviceIdType.MESH,
            )
        )
        return sends[-1]

    def local(source, target):
        position = len(locals_)
        locals_.append(pltpu.make_async_copy(source, target, local_sem.at[position]))
        return locals_[-1]

    def blocks_of(index):
        away, half = lax.div(index, 2), lax.rem(index, 2)
        far = lax.div(away + lines - 1, lines)
        at = lax.rem(row + lines - away, lines) * 2
        chosen = (at + core + half * (1 - 2 * core)) * 2
        first = far * ((at + core) * 2 + half) + (1 - far) * chosen
        second = far * ((at + 1 - core) * 2 + half) + (1 - far) * (chosen + 1)
        return first, second

    own = local(shard_ref, sw_s.at[0])
    own_over = remote(shard_ref, sw_s.at[1], sibling)
    rep = lax.axis_index("rep")
    side = lax.rem(rep, 2)
    pair = {"rep": rep + 1 - 2 * side}
    deep = block // 2
    far_moves, pair_moves, over_moves = [None, None], [None, None], [None, None]
    for away in range(1, lines):
        target = {"fsdp": lax.rem(row + away, lines) * 2 + core}
        for half in range(2):
            slot = 2 * away + half

            def here(which, over):
                at = pl.multiple_of(over * block + which * deep, deep)
                return sw_s.at[slot, pl.ds(at, deep), :]

            if half == 0:
                held = first_ref.at[away - 1]
                far_moves.append(local(held, here(side, 0)))
            else:
                held = here(side, 0)
                start = pl.multiple_of(block + side * deep, deep)
                far_moves.append(remote(shard_ref.at[pl.ds(start, deep), :], held, target))
            pair_moves.append(remote(held, here(side, 0), pair))
            over_moves.append(
                [
                    remote(held, here(side, 1), sibling),
                    remote(here(1 - side, 0), here(1 - side, 1), sibling),
                ]
            )
    ew_moves = []
    for index in range(steps):
        for i, which in enumerate(blocks_of(jnp.int32(index))):
            ew_moves.append(local(ew_ref.at[which], ew_s.at[2 * index + i]))

    near = cot_ref.shape[1]
    ow_move = local(ow_hbm, ow_ref)

    def incoming(i):
        rows = pl.ds(pl.multiple_of(i * tile, tile), tile)
        pairs = ((x_hbm.at[rows, :], x_ref.at[rows, :]), (att_hbm.at[:, rows, :], att_ref.at[:, rows, :]))
        return [
            pltpu.make_async_copy(source, target, in_sem.at[2 * i + k])
            for k, (source, target) in enumerate(pairs)
        ]

    cot_moves = [
        local(cot_ref.at[seq], cot_s.at[pl.ds(0, near), :]),
        local(far_ref, cot_s.at[pl.ds(near, length - near), :]),
    ]

    assert (len(sends), len(locals_)) == (send_sem.shape[0], local_sem.shape[0])

    def put(start, values):
        for i in range(values.shape[1] // LANES):
            at = start + i
            if group:
                at = at // group * (group + 1) + at % group
            terms_ref[at] = values[:, i * LANES : (i + 1) * LANES].astype(low)

    @pl.when(step == 0)
    def _():
        ow_move.start()
        for move in incoming(0):
            move.start()
        for move in cot_moves:
            move.start()
        for i in range(1, length // tile):
            for move in incoming(i):
                move.start()
        for move in (ew_moves[0], ew_moves[1], own):
            move.start()
        barrier = pltpu.get_barrier_semaphore()
        peers = [sibling, pair] + [
            {"fsdp": lax.rem(row + away, lines) * 2 + core} for away in range(1, lines)
        ]
        for peer in peers:
            pl.semaphore_signal(barrier, inc=1, device_id=peer, device_id_type=pl.DeviceIdType.MESH)
        pl.semaphore_wait(barrier, len(peers))
        for away in range(1, lines):
            far_moves[2 * away + 1].start()
            pair_moves[2 * away].start()
            over_moves[2 * away][0].start()
        own_over.start()

        def enter(rows):
            attended = join_planes(att_ref, rows)
            leave_low = dot_nt(attended, o1_ref[...]).astype(low)
            leave_s[rows, :] = leave_low
            branch = (
                dot_nn(attended, ow_ref[...])
                + obias_ref[...]
                + 2.0 * dot_nn(leave_low, o2_ref[...])
            )
            middle = x_ref[rows, :].astype(wide) + oscale_ref[...] * branch
            middle_s[rows, :] = middle
            normed = layer_norm(middle, gain_ref[...], shift_ref[...]).astype(low)
            normed_s[rows, :] = normed
            widen_s[rows, :] = dot_nt(normed, e1_ref[...]).astype(low)
            gfeed = (cot_s[rows, :].astype(wide) * live * fscale_ref[...]).astype(low)
            gfeed_s[rows, :] = gfeed
            gnarrow_s[rows, :] = (2.0 * dot_nt(gfeed, s2_ref[...])).astype(low)
            feed_s[rows, :] = jnp.zeros((tile, width), wide)
            gnormed_s[rows, :] = jnp.zeros((tile, width), wide)

        ow_move.wait()
        for move in cot_moves:
            move.wait()

        def enter_tile(i, carry):
            for move in incoming(i):
                move.wait()
            enter(pl.ds(pl.multiple_of(i * tile, tile), tile))
            return carry

        lax.fori_loop(0, length // tile, enter_tile, 0)
        narrow_s[...] = jnp.zeros_like(narrow_s)
        gwiden_s[...] = jnp.zeros_like(gwiden_s)

    def pass_on():
        @pl.when(step == 1)
        def _():
            for away in range(1, lines):
                near, later = 2 * away, 2 * away + 1
                far_moves[later].wait_recv()
                pair_moves[later].start()
                over_moves[later][0].start()
                pair_moves[near].wait_recv()
                over_moves[near][1].start()

        @pl.when(step == 2)
        def _():
            for away in range(1, lines):
                later = 2 * away + 1
                pair_moves[later].wait_recv()
                over_moves[later][1].start()

    for index in range(steps):
        @pl.when(step == index + 1)
        def _(index=index):
            ew_moves[2 * index].wait()
            ew_moves[2 * index + 1].wait()
            if index + 1 < steps:
                ew_moves[2 * index + 2].start()
                ew_moves[2 * index + 3].start()
                if index % 2:
                    far_moves[index + 1].start()
            if index == 0:
                own.wait()
            elif index == 1:
                own_over.wait_recv()
            else:
                if index % 2 == 0:
                    far_moves[index].wait()
                for move in over_moves[index]:
                    move.wait_recv()

    @pl.when((step > 0) & (step <= steps))
    def _():
        index = step - 1
        first, second = blocks_of(index)

        def part_of(table_ref):
            return jnp.concatenate(
                [
                    table_ref[:, pl.ds(pl.multiple_of(which * block, block), block)]
                    for which in (first, second)
                ],
                axis=1,
            )

        e2, s1, ebias = part_of(e2_ref), part_of(s1_ref), part_of(ebias_ref)
        inner, outer = chunk // 4, width // 4
        ts1_ref[...] = jnp.zeros_like(ts1_ref)
        te2_ref[...] = jnp.zeros_like(te2_ref)

        long_tile = 2 * tile

        def run(rows):
            normed, gfeed = normed_s[rows, :], gfeed_s[rows, :]
            widen_low, gnarrow = widen_s[rows, :], gnarrow_s[rows, :]
            widen_twice = widen_low * low(2.0)
            raw, made = [], []
            for n in range(5):
                if n < 4:
                    here = slice(n * inner, (n + 1) * inner)
                    held = slice(n % 2 * inner, (n % 2 + 1) * inner)
                    before = (
                        dot_nn(normed, ew_s[2 * index + n // 2, :, held])
                        + ebias[:, here]
                        + dot_nn(widen_twice, e2[:, here])
                    )
                    ghidden = dot_nt(gfeed, sw_s[index, here, :]) + dot_nn(gnarrow, s1[:, here])
                    raw.append((before, ghidden))
                if n:
                    before, ghidden = raw[n - 1]
                    ghidden = ghidden.astype(low).astype(wide)
                    scaled = before * math.sqrt(0.5)
                    share = 0.5 + 0.5 * lax.erf(scaled)
                    density = math.sqrt(0.5 / math.pi) * jnp.exp(-(scaled * scaled))
                    made.append(
                        (
                            (before * share).astype(low),
                            (ghidden * (share + before * density)).astype(low),
                        )
                    )
            hidden = jnp.concatenate([one[0] for one in made], axis=1)
            gbefore = jnp.concatenate([one[1] for one in made], axis=1)
            for n in range(4):
                there = slice(n * outer, (n + 1) * outer)
                feed_s[rows, there] += dot_nn(hidden, sw_s[index, :, there])
                gnormed_s[rows, there] += dot_nt(
                    gbefore[:, :block], ew_s[2 * index, there, :]
                ) + dot_nt(gbefore[:, block:], ew_s[2 * index + 1, there, :])
            narrow_s[rows, :] += dot_nt(hidden, s1)
            gwiden_s[rows, :] += dot_nt(gbefore, e2)
            ts1_ref[...] += dot_tn(gnarrow, hidden)
            te2_ref[...] += 2.0 * dot_tn(widen_low, gbefore)

        turns = length // long_tile

        def turn(i, carry):
            @pl.when(i == turns // 2)
            def _():
                pass_on()

            run(pl.ds(pl.multiple_of(i * long_tile, long_tile), long_tile))
            return carry

        lax.fori_loop(0, turns, turn, 0)
        block_tiles = block // LANES
        for i, which in enumerate((first, second)):
            here = slice(i * block, (i + 1) * block)
            start = 3 * tiles + which * block_tiles
            put(start, te2_ref[:, here])
            put(start + 2 * steps * block_tiles, ts1_ref[:, here])

    @pl.when(step == steps + 1)
    def _():
        o1, o2, e1, s2 = o1_ref[...], o2_ref[...], e1_ref[...], s2_ref[...]
        to1_ref[...] = jnp.zeros_like(to1_ref)
        to2_ref[...] = jnp.zeros_like(to2_ref)
        te1_ref[...] = jnp.zeros_like(te1_ref)
        ts2_ref[...] = jnp.zeros_like(ts2_ref)

        def leave(rows):
            middle = middle_s[rows, :]
            narrow_low = narrow_s[rows, :].astype(low)
            feed = feed_s[rows, :] + sbias_ref[...] + 2.0 * dot_nn(narrow_low, s2)
            result_ref[rows, :] = (live * (middle + fscale_ref[...] * feed)).astype(low)
            ts2_ref[...] += 2.0 * dot_tn(narrow_low, gfeed_s[rows, :])
            gwiden = (2.0 * gwiden_s[rows, :]).astype(low)
            te1_ref[...] += dot_tn(gwiden, normed_s[rows, :])
            gnormed = gnormed_s[rows, :] + dot_nn(gwiden, e1)
            gmiddle = cot_s[rows, :].astype(wide) * live + layer_norm_back(
                gnormed, middle, gain_ref[...]
            )
            gmid_ref[rows, :] = gmiddle
            gbranch = (gmiddle * oscale_ref[...]).astype(low)
            to2_ref[...] += 2.0 * dot_tn(leave_s[rows, :], gbranch)
            gleave = (2.0 * dot_nt(gbranch, o2)).astype(low)
            to1_ref[...] += dot_tn(gleave, join_planes(att_ref, rows))
            gatt = (dot_nt(gbranch, ow_ref[...]) + dot_nn(gleave, o1)).astype(low)
            for i in range(tiles):
                gatt_ref[i, rows, :] = gatt[:, i * LANES : (i + 1) * LANES]

        def outgoing(i):
            rows = pl.ds(pl.multiple_of(i * tile, tile), tile)
            pairs = (
                (result_ref.at[rows, :], result_out.at[rows, :]),
                (gmid_ref.at[rows, :], gmid_out.at[rows, :]),
                (gatt_ref.at[:, rows, :], gatt_out.at[:, rows, :]),
            )
            return [
                pltpu.make_async_copy(source, target, out_sem.at[3 * i + k])
                for k, (source, target) in enumerate(pairs)
            ]

        def leave_tile(i, carry):
            leave(pl.ds(pl.multiple_of(i * tile, tile), tile))
            for copy in outgoing(i):
                copy.start()
            return carry

        lax.fori_loop(0, length // tile, leave_tile, 0)
        put(0, to1_ref[...])
        put(tiles, to2_ref[...])
        put(2 * tiles, te1_ref[...])
        put(3 * tiles + 4 * steps * (block // LANES), ts2_ref[...])
        if group:
            for i in range(terms_ref.shape[0] // (group + 1)):
                kind = jnp.full(terms_ref.shape[1:], set_ref[seq], jnp.int32).astype(wide)
                terms_ref[i * (group + 1) + group] = kind.astype(low)
        for i in range(length // tile):
            for copy in outgoing(i):
                copy.wait()
        for copy in sends:
            copy.wait_send()


def feed_forward(sizes, sets, lives, values, attended, cotangent, far, obias, oscale, gain, shift, ebias,
                 sbias, fscale, oweight, eweight, shrink, first, o1, o2, e1, e2, s1, s2, group, tile=256):
    length, width = values.shape
    rank, hidden = e2.shape
    steps = sizes["fsdp"]
    chunk = hidden // steps
    once = pl.Buffered(1)

    def resident(shape):
        return pl.BlockSpec(shape, lambda i: (0,) * len(shape), pipeline_mode=once)

    anywhere = pl.BlockSpec(memory_space=pl.ANY)
    scalars = pl.BlockSpec(memory_space=pltpu.SMEM)
    vector = resident((1, width))
    table, table_wide = resident((rank, width)), resident((rank, hidden))
    term_tiles = (4 * width + 2 * hidden) // LANES
    if group:
        term_tiles += term_tiles // group
    terms = (term_tiles, rank, LANES)
    flops = 2 * length * width * (4 * hidden + 2 * width)
    remotes = 1 + 7 * (steps - 2) // 2
    return pl.pallas_call(
        functools.partial(feed_kernel, sizes=sizes, tile=tile, group=group),
        grid=(steps + 2,),
        in_specs=[
            scalars,
            scalars,
            anywhere,
            anywhere,
            anywhere,
            anywhere,
            vector,
            vector,
            vector,
            vector,
            resident((1, hidden)),
            vector,
            vector,
            anywhere,
            anywhere,
            anywhere,
            anywhere,
            table,
            table,
            table,
            table_wide,
            table_wide,
            table,
        ],
        out_specs=[anywhere, anywhere, anywhere, resident(terms)],
        scratch_shapes=[
            pltpu.VMEM((length, width), low),
            pltpu.VMEM(attended.shape, low),
            pltpu.VMEM((width, width), low),
            pltpu.VMEM((length, width), wide),
            pltpu.VMEM((length, width), low),
            pltpu.VMEM((length, width), low),
            pltpu.VMEM((length, width), wide),
            pltpu.VMEM((length, width), wide),
            pltpu.VMEM(eweight.shape, low),
            pltpu.VMEM((steps, chunk, width), low),
            pltpu.VMEM((length, width), low),
            pltpu.VMEM((length, width), low),
            pltpu.VMEM((length, width), wide),
            pltpu.VMEM(attended.shape, low),
            pltpu.VMEM((length, rank), low),
            pltpu.VMEM((length, rank), low),
            pltpu.VMEM((length, rank), low),
            pltpu.VMEM((length, rank), wide),
            pltpu.VMEM((length, rank), wide),
            pltpu.VMEM((rank, width), wide),
            pltpu.VMEM((rank, width), wide),
            pltpu.VMEM((rank, width), wide),
            pltpu.VMEM((rank, chunk), wide),
            pltpu.VMEM((rank, chunk), wide),
            pltpu.VMEM((rank, width), wide),
            pltpu.SemaphoreType.DMA((remotes,)),
            pltpu.SemaphoreType.DMA((remotes,)),
            pltpu.SemaphoreType.DMA((4 + 2 * steps + (steps - 2) // 2,)),
            pltpu.SemaphoreType.DMA((3 * (length // tile),)),
            pltpu.SemaphoreType.DMA((2 * (length // tile),)),
        ],
        out_shape=[
            jax.ShapeDtypeStruct((length, width), low),
            jax.ShapeDtypeStruct((length, width), wide),
            jax.ShapeDtypeStruct(attended.shape, low),
            jax.ShapeDtypeStruct(terms, low),
        ],
        compiler_params=pltpu.CompilerParams(
            vmem_limit_bytes=62 << 20, collective_id=2, has_side_effects=True
        ),
        cost_estimate=pl.CostEstimate(
            flops=flops,
            bytes_accessed=2 * width * (2 * hidden + width) + 14 * length * width,
            transcendentals=2 * length * hidden,
        ),
        name="feed",
    )(sets, lives, values, attended, cotangent, far, obias, oscale, gain, shift, ebias, sbias, fscale,
      oweight, eweight, shrink, first, o1, o2, e1, e2, s1, s2)


def back_kernel(q_ref, k_ref, v_ref, g_ref, o_ref, r_ref, lse_ref, result_ref, early_ref,
                weight_ref, x_ref, gmid_ref, normed_ref, low_ref, gain_ref, first_ref, second_ref,
                out_ref, grad_ref, early_out, late_out,
                q_cols, g_cols, key_sum, value_sum, joined_s, weight_s, x_s, gmid_s, normed_s,
                result_s, home_s, genter_s, terms_s, early_in, late_in, early_sum, late_sum,
                send_sem, recv_sem, swap_send, swap_recv, local_sem, *, sizes, summing,
                tile):
    step = pl.program_id(0)
    steps = pl.num_programs(0) - 1
    count, reps, lines = sizes["seq"], sizes["rep"], sizes["fsdp"] // 2
    devices = count * reps * lines * 2
    rep, line = lax.axis_index("rep"), lax.axis_index("fsdp")
    seq = lax.axis_index("seq")
    core = lax.rem(line, 2)
    row = lax.div(line, 2)
    sets = early_sum.shape[0]
    part = out_ref.shape[1]
    sends, locals_ = [], []

    def place(core_at, seq_at, row_at, rep_at):
        return ((core_at * count + seq_at) * lines + row_at) * reps + rep_at

    mine = place(core, seq, row, rep)

    def remote(source, target, device):
        position = len(sends)
        sends.append(
            pltpu.make_async_remote_copy(
                src_ref=source,
                dst_ref=target,
                send_sem=send_sem.at[position],
                recv_sem=recv_sem.at[position],
                device_id=device,
                device_id_type=pl.DeviceIdType.MESH,
            )
        )
        return sends[-1]

    def local(source, target):
        position = len(locals_)
        locals_.append(pltpu.make_async_copy(source, target, local_sem.at[position]))
        return locals_[-1]

    def begin(copies):
        for copy in copies:
            copy.start()

    def arrived(copies):
        for copy in copies:
            copy.wait_recv()

    def other(offset):
        spot = lax.rem(mine + offset, devices)
        rep_at = lax.rem(spot, reps)
        row_at = lax.rem(lax.div(spot, reps), lines)
        seq_at = lax.rem(lax.div(spot, reps * lines), count)
        core_at = lax.div(spot, reps * lines * count)
        return spot, {"rep": rep_at, "fsdp": row_at * 2 + core_at, "seq": seq_at}

    def swap(phase, offset, source, target):
        spot, device = other(offset)
        size = source.shape[0] // devices
        return pltpu.make_async_remote_copy(
            src_ref=source.at[pl.ds(spot * size, size)],
            dst_ref=target.at[offset],
            send_sem=swap_send.at[phase, offset],
            recv_sem=swap_recv.at[phase, offset],
            device_id=device,
            device_id_type=pl.DeviceIdType.MESH,
        )

    def each_other(body):
        def turn(offset, carry):
            body(offset)
            return carry

        lax.fori_loop(1, devices, turn, 0)

    def add_by_set(source, kinds, target):
        for index in range(target.shape[1]):
            def turn(offset, totals):
                kind = kinds[offset, kinds.shape[1] - 1].astype(wide)
                piece = source[offset, index].astype(wide)
                return tuple(
                    total + jnp.where(kind == float(which), piece, 0.0)
                    for which, total in enumerate(totals)
                )

            zero = jnp.zeros(target.shape[2:], wide)
            totals = lax.fori_loop(0, devices, turn, (zero,) * sets)
            for which, total in enumerate(totals):
                target[which, index] = total.astype(low)

    def stages(piece, whole):
        along_rep = [{"rep": lax.rem(rep + s, reps)} for s in range(1, reps)]
        along_row = [{"fsdp": lax.rem(row + s, lines) * 2 + core} for s in range(1, lines)]
        along_seq = [{"seq": lax.rem(seq + s, count)} for s in range(1, count)]
        ones, others = pl.ds(0, sets // 2), pl.ds(sets // 2, sets // 2)
        every = pl.ds(0, sets)

        def send(start, size, which, targets):
            block = whole.at[pl.ds(start, size), which]
            return [remote(block, block, target) for target in targets]

        line_start = place(core, seq, row, 0)
        moves = [send(mine, 1, every, along_rep)]
        moves.append(
            send(line_start, reps, ones, along_row) + send(line_start, reps, others, along_seq)
        )
        last = send(place(core, seq, 0, 0), reps * lines, ones, along_seq)
        for s in range(count):
            last += send(place(core, s, row, 0), reps, others, along_row)
        moves.append(last)
        moves.append(
            send(place(core, 0, 0, 0), reps * lines * count, every, [{"fsdp": line + 1 - 2 * core}])
        )
        return local(piece, whole.at[mine]), moves

    def late_stages(piece, whole):
        every = pl.ds(0, sets)

        def send(start, size, targets):
            block = whole.at[pl.ds(start, size), every]
            return [remote(block, block, target) for target in targets]

        moves = [send(mine, 1, [{"seq": lax.rem(seq + s, count)} for s in range(1, count)]), [], []]
        for s in range(count):
            moves[1] += send(
                place(core, s, row, rep), 1, [{"rep": lax.rem(rep + i, reps)} for i in range(1, reps)]
            )
            moves[2] += send(
                place(core, s, row, 0),
                reps,
                [{"fsdp": lax.rem(row + i, lines) * 2 + core} for i in range(1, lines)],
            )
        moves.append(
            send(place(core, 0, 0, 0), reps * lines * count, [{"fsdp": line + 1 - 2 * core}])
        )
        return local(piece, whole.at[mine]), moves

    if summing:
        early_keep, early_moves = stages(early_sum, early_out)
        late_keep, late_moves = late_stages(late_sum, late_out)
    around = [lax.rem(seq + shift, count) for shift in range(1, count)]
    result_moves = [
        remote(result_s.at[pl.ds(shift * part, part), :], out_ref.at[seq], {"seq": to})
        for shift, to in enumerate(around, 1)
    ]
    result_load = local(result_ref, result_s)
    result_own = local(result_s.at[pl.ds(0, part), :], out_ref.at[seq])
    short = min(tile, part)
    grad_moves = [
        [
            [
                remote(
                    home_s.at[pl.ds(shift * part + start, short), :],
                    grad_ref.at[seq, pl.ds(start, short), :],
                    {"seq": to},
                )
            ]
            for start in range(0, part, short)
        ]
        for shift, to in enumerate(around, 1)
    ]
    grad_own = local(home_s.at[pl.ds(0, part), :], grad_ref.at[seq])
    loads = [
        local(weight_ref, weight_s),
        local(x_ref, x_s),
        local(gmid_ref, gmid_s),
        local(normed_ref, normed_s),
    ]
    keep_sem = local_sem.at[len(locals_)]

    assert len(sends) == send_sem.shape[0] and len(locals_) < local_sem.shape[0]

    @pl.when(step == 0)
    def _():
        result_load.start()
        barrier = pltpu.get_barrier_semaphore()

        def greet(device):
            pl.semaphore_signal(
                barrier, inc=1, device_id=device, device_id_type=pl.DeviceIdType.MESH
            )

        if summing:
            each_other(lambda offset: greet(other(offset)[1]))
            pl.semaphore_wait(barrier, devices - 1)
            size = early_ref.shape[0] // devices
            keep = pltpu.make_async_copy(
                early_ref.at[pl.ds(mine * size, size)], early_in.at[0], keep_sem
            )
            keep.start()
            each_other(lambda offset: swap(0, offset, early_ref, early_in).start())
            keep.wait()
        else:
            for to in around:
                greet({"seq": to})
            pl.semaphore_wait(barrier, count - 1)
        result_load.wait()
        begin(result_moves)
        result_own.start()

    if summing:
        @pl.when(step == 3)
        def _():
            each_other(lambda offset: swap(0, offset, early_ref, early_in).wait_recv())
            add_by_set(early_in, early_in, early_sum)
            early_keep.start()
            early_keep.wait()
            begin(early_moves[0])

        for number, at in ((1, 5), (2, 7)):
            @pl.when(step == at)
            def _(number=number):
                arrived(early_moves[number - 1])
                begin(early_moves[number])

    for number, load in enumerate(loads):
        @pl.when(step == number + 2)
        def _(load=load):
            load.start()

    @pl.when(step < steps)
    def _():
        attend_back_pair(
            q_ref.at[0], k_ref.at[0], v_ref.at[0], g_ref.at[0], o_ref.at[0], r_ref.at[0],
            lse_ref.at[0], joined_s,
            pl.multiple_of(step * LANES, LANES), q_cols, g_cols, key_sum, value_sum, tile,
        )

    @pl.when(step == steps)
    def _():
        first = first_ref[...]
        width = x_s.shape[1]
        planes = joined_s.shape[0]
        tiles = width // LANES
        length = x_s.shape[0]
        chunk = weight_s.shape[2]
        per = width // chunk
        seconds = [
            second_ref[:, p * width : (p + 1) * width] for p in range(planes)
        ]
        for load in loads:
            load.wait()

        def enter_back(rows):
            genter = dot_nt(joined_s[0, rows, :], seconds[0])
            for p in range(1, planes):
                genter += dot_nt(joined_s[p, rows, :], seconds[p])
            genter_s[rows, :] = (2.0 * genter).astype(low)

        for_rows(length, tile, enter_back)

        def leave(rows):
            gnormed = dot_nn(genter_s[rows, :], first)
            for p in range(planes):
                for i in range(per):
                    gnormed += dot_nt(
                        joined_s[p, rows, i * chunk : (i + 1) * chunk], weight_s[p * per + i]
                    )
            back = layer_norm_back(gnormed, x_s[rows, :].astype(wide), gain_ref[...])
            home_s[rows, :] = (gmid_s[rows, :] + back).astype(low)

        for p in range(planes + 1):
            if p == 0:
                values = dot_tn(genter_s[...], normed_s[...]).astype(low)
            else:
                values = (2.0 * dot_tn(low_ref[...], joined_s[p - 1])).astype(low)
            for i in range(tiles):
                terms_s[p * tiles + i] = values[:, i * LANES : (i + 1) * LANES]
        if summing:
            size = terms_s.shape[0] // devices
            keep = pltpu.make_async_copy(
                terms_s.at[pl.ds(mine * size, size)], late_in.at[0], keep_sem
            )
            keep.start()
            each_other(lambda offset: swap(1, offset, terms_s, late_in).start())
            keep.wait()
        else:
            keep = pltpu.make_async_copy(terms_s, late_out, keep_sem)
            keep.start()
            keep.wait()
        far_rows = list(range(part, length, short))

        def run_far():
            start = far_rows.pop(0)
            for_rows(short, short, leave, start)
            return grad_moves[start // part - 1][(start % part) // short]

        ready = run_far()
        if summing:
            each_other(lambda offset: swap(1, offset, terms_s, late_in).wait_recv())
            add_by_set(late_in, early_in, late_sum)
            late_keep.start()
            late_keep.wait()
            begin(late_moves[0])
        begin(ready)
        if summing:
            arrived(early_moves[2])
            begin(early_moves[3])
        while far_rows:
            begin(run_far())
        number = 1
        for start in range(0, part, short):
            if summing and number < 3:
                arrived(late_moves[number - 1])
                begin(late_moves[number])
                number += 1
            for_rows(short, short, leave, start)
        grad_own.start()
        if summing:
            while number < 4:
                arrived(late_moves[number - 1])
                begin(late_moves[number])
                number += 1
            arrived(late_moves[3])
            arrived(early_moves[3])
        arrived(result_moves)
        for moves in grad_moves:
            for pieces in moves:
                arrived(pieces)
        result_own.wait()
        grad_own.wait()
        for copy in sends:
            copy.wait_send()
        if summing:
            each_other(lambda offset: swap(0, offset, early_ref, early_in).wait_send())
            each_other(lambda offset: swap(1, offset, terms_s, late_in).wait_send())


def back(sizes, summing, set_count, joined, grads, attended, rest, logsum, result, early, weight,
         values, gmiddle, normed, enter_low, gain, first, second, tile=256):
    length, width = values.shape
    count = sizes["seq"]
    devices = count * sizes["rep"] * sizes["fsdp"]
    rank = enter_low.shape[1]
    pairs = width // LANES
    late_tiles = 4 * pairs
    if summing:
        early_size, late_size = early.shape[0] // devices, late_tiles // devices
        early_shape = (devices, set_count, early_size - 1, rank, LANES)
        late_shape = (devices, set_count, late_size, rank, LANES)
    else:
        early_size, late_size = 2, 1
        early_shape, late_shape = (1, rank, LANES), (late_tiles, rank, LANES)
    part = length // count
    once = pl.Buffered(1)
    anywhere = pl.BlockSpec(memory_space=pl.ANY)

    def resident(shape):
        return pl.BlockSpec(shape, lambda i: (0,) * len(shape), pipeline_mode=once)

    def plane(start):
        return pl.BlockSpec(
            (1, length, LANES), lambda i: (jnp.minimum(i, pairs - 1) + start, 0, 0)
        )

    lines = sizes["fsdp"] // 2
    spread = sizes["rep"] - 1 + (lines - 1) * (1 + count) + 2 * (count - 1) + 1
    late_spread = (count - 1) + count * (sizes["rep"] - 1 + lines - 1) + 1
    remotes = (spread + late_spread if summing else 0) + (count - 1) * (1 + part // min(tile, part))
    home = jax.ShapeDtypeStruct((count, part, width), low)
    return pl.pallas_call(
        functools.partial(back_kernel, sizes=sizes, summing=summing, tile=tile),
        grid=(pairs + 1,),
        in_specs=[
            plane(0),
            plane(pairs),
            plane(2 * pairs),
            plane(0),
            plane(0),
            plane(0),
            plane(0),
            anywhere,
            anywhere,
            anywhere,
            anywhere,
            anywhere,
            anywhere,
            resident((length, rank)),
            resident((1, width)),
            resident(first.shape),
            resident(second.shape),
        ],
        out_specs=[anywhere] * 4,
        out_shape=[
            home,
            home,
            jax.ShapeDtypeStruct(early_shape, low),
            jax.ShapeDtypeStruct(late_shape, low),
        ],
        scratch_shapes=[
            pltpu.VMEM((LANES, length), low),
            pltpu.VMEM((LANES, length), low),
            pltpu.VMEM((LANES, length), wide),
            pltpu.VMEM((LANES, length), wide),
            pltpu.VMEM((3, length, width), low),
            pltpu.VMEM(weight.shape, low),
            pltpu.VMEM((length, width), low),
            pltpu.VMEM((length, width), wide),
            pltpu.VMEM((length, width), low),
            pltpu.VMEM((length, width), low),
            pltpu.VMEM((length, width), low),
            pltpu.VMEM((length, rank), low),
            pltpu.VMEM((late_tiles, rank, LANES), low),
            pltpu.VMEM((devices, early_size, rank, LANES), low),
            pltpu.VMEM((devices, late_size, rank, LANES), low),
            pltpu.VMEM((set_count, early_size - 1, rank, LANES), low),
            pltpu.VMEM((set_count, late_size, rank, LANES), low),
            pltpu.SemaphoreType.DMA((remotes,)),
            pltpu.SemaphoreType.DMA((remotes,)),
            pltpu.SemaphoreType.DMA((2, devices)),
            pltpu.SemaphoreType.DMA((2, devices)),
            pltpu.SemaphoreType.DMA((10,)),
        ],
        compiler_params=pltpu.CompilerParams(
            vmem_limit_bytes=60 << 20, collective_id=1, has_side_effects=True
        ),
        cost_estimate=pl.CostEstimate(
            flops=40 * length * length * width + 6 * length * width * width,
            bytes_accessed=40 * length * width,
            transcendentals=length * length * width // HEAD_DIM,
        ),
        name="back",
    )(joined, joined, joined, grads, attended, rest, logsum, result, early, weight, values,
      gmiddle, normed, enter_low, gain, first, second)


def lay_out_kernel(images, sources, kept, targets, *, tiles):
    targets = list(targets)
    for image, out in zip(images, kept):
        out[...] = image[...]
    for source, widths in zip(sources, tiles):
        size = source.shape[2]
        position = 0
        for width in widths:
            target = targets.pop(0)
            for i in range(width):
                piece = source[position // size, :, position % size]
                target[:, :, i * LANES : (i + 1) * LANES] = piece.astype(wide)
                position += 1


def lay_out(images, sources, widths, together=2):
    set_count = sources[0].shape[1]
    rank = sources[0].shape[3]
    tiles = tuple(tuple(width // LANES for width in group) for group in widths)
    flat = [width for group in widths for width in group]
    steps = set_count // together
    count, part, size = images[0].shape
    image = pl.BlockSpec((count, part // steps, size), lambda i: (0, i, 0))
    return pl.pallas_call(
        functools.partial(lay_out_kernel, tiles=tiles),
        grid=(steps,),
        in_specs=[
            [image] * len(images),
            [
                pl.BlockSpec(
                    (source.shape[0], together, source.shape[2], rank, LANES),
                    lambda i: (0, i, 0, 0, 0),
                )
                for source in sources
            ],
        ],
        out_specs=[
            [image] * len(images),
            [pl.BlockSpec((together, rank, width), lambda i: (i, 0, 0)) for width in flat],
        ],
        out_shape=[
            [jax.ShapeDtypeStruct(one.shape, one.dtype) for one in images],
            [jax.ShapeDtypeStruct((set_count, rank, width), wide) for width in flat],
        ],
        compiler_params=pltpu.CompilerParams(vmem_limit_bytes=60 << 20),
        cost_estimate=pl.CostEstimate(
            flops=0, bytes_accessed=6 * set_count * rank * sum(flat), transcendentals=0
        ),
        name="lay_out",
    )(list(images), list(sources))


def sum_by_set(terms, choose, axes, devices):
    tiles, rank, _ = terms.shape
    sets = choose.shape[1]
    pieces = lax.all_to_all(terms.reshape(devices, -1), axes, 0, 0, tiled=True)
    summed = jnp.einsum("ns,nx->sx", choose, pieces, preferred_element_type=wide).astype(low)
    whole = lax.all_gather(summed, axes, axis=1, tiled=True)
    whole = whole.reshape(sets, tiles, rank, LANES)
    return whole.transpose(0, 2, 1, 3).reshape(sets, rank, tiles * LANES).astype(wide)


def shards(
    tokens,
    cotangent,
    adapter_set,
    image_live,
    first_gain,
    first_shift,
    inproj_weight,
    inproj_bias,
    outproj_weight,
    outproj_bias,
    attend_scale,
    second_gain,
    second_shift,
    expand_weight,
    expand_bias,
    shrink_weight,
    shrink_bias,
    feedfwd_scale,
    inproj_first,
    inproj_second,
    outproj_first,
    outproj_second,
    expand_first,
    expand_second,
    shrink_first,
    shrink_second,
    *,
    sizes,
):
    count = sizes["seq"]
    axes = ("rep", "fsdp", "seq")
    devices = sizes["rep"] * sizes["fsdp"] * count
    set_count = inproj_first.shape[0]
    def row(vector):
        return vector.reshape(1, vector.shape[0])

    def flip(table):
        return jnp.swapaxes(table, 1, 2)

    (
        values, far, whole_inproj, whole_outproj, whole_expand, far_shrink, normed,
        joined, enter_low, picked, attended, rest, logsum,
    ) = front(
        sizes, adapter_set, tokens, cotangent, row(first_gain), row(first_shift), row(inproj_bias),
        (inproj_weight, outproj_weight, expand_weight, shrink_weight),
        (
            flip(inproj_first), inproj_second, flip(outproj_first), outproj_second,
            flip(expand_first), expand_second, flip(shrink_first), shrink_second,
        ),
    )
    enter_first, enter_second, *feed_tables = picked
    late_tables = (inproj_first, inproj_second)
    early_tables = (
        outproj_first, outproj_second, expand_first, expand_second, shrink_first, shrink_second
    )
    rank = inproj_second.shape[1]
    widths = [
        [table.shape[1] * table.shape[2] // rank for table in tables]
        for tables in (late_tables, early_tables)
    ]
    tiles = [sum(group) // LANES for group in widths]
    summing = all(tile % devices == 0 for tile in tiles)
    result, gmiddle, gattended, early = feed_forward(
        sizes, adapter_set, image_live, values, attended, cotangent, far, row(outproj_bias),
        row(attend_scale), row(second_gain), row(second_shift), row(expand_bias), row(shrink_bias),
        row(feedfwd_scale), whole_outproj, whole_expand, shrink_weight, far_shrink, *feed_tables,
        tiles[1] // devices if summing else 0,
    )
    block_output, input_grad, early_sums, late_sums = back(
        sizes, summing, set_count, joined, gattended, attended, rest, logsum, result, early,
        whole_inproj, values, gmiddle, normed, enter_low, row(first_gain), enter_first,
        enter_second,
    )
    if summing:
        (block_output, input_grad), tables = lay_out(
            (block_output, input_grad), (late_sums, early_sums), widths
        )
    else:
        index = lax.dynamic_slice_in_dim(adapter_set, lax.axis_index("seq"), 1)
        sets = lax.all_gather(index, axes, axis=0, tiled=True)
        choose = (sets[:, None] == jnp.arange(set_count)[None, :]).astype(low)
        tables = []
        for terms, group in ((late_sums, widths[0]), (early, widths[1])):
            whole = sum_by_set(terms, choose, axes, devices)
            start = 0
            for size in group:
                tables.append(whole[:, :, start : start + size])
                start += size
    tables = [flip(table) if i % 2 == 0 else table for i, table in enumerate(tables)]
    return (block_output, input_grad, *tables)


def solution(mesh):
    images = P(("rep", "fsdp"), "seq", None)
    slots = P(("rep", "fsdp"))
    rows = P("fsdp", None)
    whole = P()
    return jax.shard_map(
        functools.partial(shards, sizes=dict(mesh.shape)),
        mesh=mesh,
        in_specs=(
            images, images, slots, slots, whole, whole, rows, whole, rows, whole, whole, whole,
            whole, rows, whole, rows, whole, whole, whole, whole, whole, whole, whole, whole, whole,
            whole,
        ),
        out_specs=(images, images) + (whole,) * 8,
        check_vma=False,
    )
```
